256 devices in a mesh: row: 64 (over y_lo, z, x), width: 4 (over y_hi, core).
Axes of the slice: x: 4, y: 4 (y_hi: 2, y_lo: 2; y = y_hi * 2 + y_lo), z: 8, core: 2. Of those that a mesh axis runs over, the one named last changes fastest.
Arguments:
- image_learner: bfloat16 [16384, 1152], P('row', 'width'), may hold values from -24 to 24
- image_reference: bfloat16 [16384, 1152], P('row', 'width'), may hold values from -24 to 24
- text_learner: bfloat16 [16384, 1152], P('row', 'width'), may hold values from -24 to 24
- text_reference: bfloat16 [16384, 1152], P('row', 'width'), may hold values from -24 to 24
Outputs:
- image_score: float32 [16384], P(('row', 'width'))
- text_score: float32 [16384], P(('row', 'width'))
The draws below stay inside these ranges and needn't reach their ends.
All inputs are finite; a program needn't handle non-finite values.
Results may differ from the reference program's by a relative error of at most 0.0016.
Values may be sent and summed in bfloat16 or wider, within the bound.
No kernel may reach another device: no remote copies, remote signals or barrier semaphores. Data moves between devices by JAX's collectives and lax.ppermute only.
A program may use at most 64 MiB of HBM per device.

```python
import jax
import jax.numpy as jnp
from jax import lax

D = 1152
ROWS_DEV = 256
TOTAL = 16384


def shared_parts(key):
    cluster_key, center_key, latent_key, member_key, weight_key = jax.random.split(key, 5)
    clusters = max(TOTAL // 256, 4)
    mates = max(TOTAL // 8, 2)
    cluster_of = jax.random.randint(cluster_key, (TOTAL,), 0, clusters)
    centers = jax.random.normal(center_key, (clusters, D), jnp.float32)
    latent = jax.random.normal(latent_key, (mates, D), jnp.float32)
    member_of = jax.random.randint(member_key, (TOTAL,), 0, mates)
    weight = jax.random.uniform(weight_key, (TOTAL, 1), jnp.float32, 0.2, 1.3)
    return (weight * centers[cluster_of], latent[member_of])


def finish(key, grouped, paired, low, high, noise):
    strength = jax.random.uniform(key, (TOTAL, 1), jnp.float32, low, high)
    value = grouped + strength * paired + noise
    return jnp.clip(value, -24.0, 24.0).astype(jnp.bfloat16)


def draw_any(key, tag, low, high):
    grouped, paired = shared_parts(jax.random.fold_in(key, 7))
    key = jax.random.fold_in(key, tag)
    strength_key, noise_key = jax.random.split(key, 2)
    noise = jax.random.normal(noise_key, (TOTAL, D), jnp.float32)
    return finish(strength_key, grouped, paired, low, high, noise)


def draw_image_learner(key, part):
    return draw_any(key, 11, 0.6, 1.2)


def draw_image_reference(key, part):
    return draw_any(key, 12, 0.8, 1.2)


def draw_text_learner(key, part):
    return draw_any(key, 13, 0.0, 1.4)


def draw_text_reference(key, part):
    return draw_any(key, 14, 0.5, 1.5)


def setup_inputs(seed: int = 0) -> dict:
    splits = jax.random.split(jax.random.key(seed), 5)
    image_learner = draw_image_learner(jax.random.fold_in(splits[4], 71), 0)
    image_reference = draw_image_reference(jax.random.fold_in(splits[4], 71), 0)
    text_learner = draw_text_learner(jax.random.fold_in(splits[4], 71), 0)
    text_reference = draw_text_reference(jax.random.fold_in(splits[4], 71), 0)
    return dict(image_learner=image_learner, image_reference=image_reference, text_learner=text_learner, text_reference=text_reference)


def normalize(x):
    wide = x.astype(jnp.float32)
    total = lax.optimization_barrier(jnp.sum(wide * wide, axis=1, keepdims=True))
    return (wide * lax.rsqrt(total + 1e-06)).astype(jnp.bfloat16)

def reference(image_learner, image_reference, text_learner, text_reference):
    image_l = normalize(image_learner)
    image_r = normalize(image_reference)
    text_l = normalize(text_learner)
    text_r = normalize(text_reference)
    count = image_l.shape[0]
    blocks = count // ROWS_DEV
    column_index = jnp.arange(count, dtype=jnp.int32)

    def tile(columns, block):
        start = (block * ROWS_DEV).astype(jnp.int32)
        part_l = lax.dynamic_slice_in_dim(image_l, start, ROWS_DEV, 0)
        part_r = lax.dynamic_slice_in_dim(image_r, start, ROWS_DEV, 0)
        logit_l = 40.0 * jnp.dot(part_l, text_l.T, preferred_element_type=jnp.float32) - 2.0
        logit_r = 20.0 * jnp.dot(part_r, text_r.T, preferred_element_type=jnp.float32) - 1.0
        row_index = start + jnp.arange(ROWS_DEV, dtype=jnp.int32)
        label = jnp.where(row_index[:, None] == column_index[None, :], jnp.float32(1.0), jnp.float32(-1.0))
        gap = jax.nn.softplus(-label * logit_l) - jax.nn.softplus(-label * logit_r)
        return (columns + lax.optimization_barrier(jnp.sum(gap, axis=0)), lax.optimization_barrier(jnp.sum(gap, axis=1)))
    columns, rows = lax.scan(tile, jnp.zeros((count,), jnp.float32), jnp.arange(blocks, dtype=jnp.int32))
    return (rows.reshape(-1) / count, columns / count)
```

```python
import functools

import jax
import jax.numpy as jnp
import numpy as np
from jax import lax
from jax.experimental import pallas as pl
from jax.experimental.pallas import tpu as pltpu

AXES = ("row", "width")
Y, Z, X, H, C = 2, 8, 4, 2, 2
RING = 8
ROWS = 256
HALF = 128
DEPTH = 1152
QUARTER = 288
TOTAL = 16384
LOG2E = 1.4426950408889634
SLOT = (0, 2, 4, 6, 7, 5, 3, 1)


def device(y, z, x, h, c):
    return (((y * Z + z) * X + x) * H + h) * C + c


def place(p):
    p %= RING
    return (0, p) if p < X else (1, RING - 1 - p)


def ring_route(d):
    route = []
    for y in range(Y):
        for z in range(Z):
            for x in range(X):
                ny, nx = place((x if y == 0 else RING - 1 - x) + d)
                for h in range(H):
                    route.append((device(y, z, x, h, 0), device(y, (z + d) % Z, x, h, 0)))
                    route.append((device(y, z, x, h, 1), device(ny, z, nx, h, 1)))
    return route


AHEAD, BACK = ring_route(1), ring_route(-1)
CORES = [(i, i ^ 1) for i in range(Y * Z * X * H * C)]
HALVES = [(i, i ^ 2) for i in range(Y * Z * X * H * C)]
GROUPS = [
    [device(y, z, x, h, 0) for z in range(Z) for h in range(H)] for y in range(Y) for x in range(X)
] + [
    [device(*(place(p)[0], z, place(p)[1]), h, 1) for p in range(RING) for h in range(H)]
    for z in range(Z)
]


def send(x, route):
    return lax.ppermute(x, AXES, route)


def prep_kernel(counts, *refs):
    ins, out, scr = refs[:-2], refs[-2], refs[-1]
    at = 0
    for b, n in enumerate(counts):
        parts = ins[at : at + n]
        at += n
        acc = jnp.zeros((16, ROWS), jnp.float32)
        for part in parts:
            for r in range(0, part.shape[0], 16):
                v = part[r : r + 16, :].astype(jnp.float32)
                acc = acc + v * v
        inv = lax.rsqrt(jnp.sum(acc, axis=0, keepdims=True) + 1e-06)
        off = 0
        for part in parts:
            for r in range(0, part.shape[0], 16):
                v = part[r : r + 16, :].astype(jnp.float32)
                scr[off + r : off + r + 16, :] = (v * inv).astype(jnp.bfloat16)
            off += part.shape[0]
        for k in range(0, DEPTH, 128):
            out[b, :, k : k + 128] = scr[k : k + 128, :].T


def prep(blocks):
    counts = tuple(len(b) for b in blocks)
    n = len(blocks)
    return pl.pallas_call(
        functools.partial(prep_kernel, counts),
        out_shape=jax.ShapeDtypeStruct((n, ROWS, DEPTH), jnp.bfloat16),
        scratch_shapes=[pltpu.VMEM((DEPTH, ROWS), jnp.bfloat16)],
        compiler_params=pltpu.CompilerParams(vmem_limit_bytes=16 * 2**20),
        cost_estimate=pl.CostEstimate(
            flops=4 * n * ROWS * DEPTH, bytes_accessed=4 * n * ROWS * DEPTH, transcendentals=0
        ),
        name="prep",
    )(*[p for b in blocks for p in b])


def tile_kernel(sizes, first_new, with_diag, ints, floats, *refs):
    n = len(sizes)
    us, gs = refs[:n], refs[n : 2 * n]
    u_in, g_in, u_out, g_out, u_scr, g_scr = refs[2 * n :]
    where = [(a, b) for a in range(n) for b in range(sizes[a])]
    slots = len(where)
    core = ints[0]
    scale, shift = floats[0], floats[1]
    u_scr[...] = jnp.zeros_like(u_scr)
    g_scr[...] = jnp.zeros_like(g_scr)

    def part(refs_, s, start):
        a, b = where[s]
        return refs_[a][b, pl.ds(start, HALF), :]

    def block(hu, u_slots, g_slots):
        g_start = pl.multiple_of((core ^ hu) * HALF, HALF)
        left = jnp.concatenate([part(us, s, hu * HALF) for s in u_slots], axis=0)
        right = jnp.concatenate([part(gs, s, g_start) for s in g_slots], axis=0)
        sums = lax.dot_general(
            left, right, (((1,), (1,)), ((), ())), preferred_element_type=jnp.float32
        )
        for i, su in enumerate(u_slots):
            for j, sg in enumerate(g_slots):
                v = sums[i * HALF : (i + 1) * HALF, j * HALF : (j + 1) * HALF] * scale + shift
                if with_diag and su == 0 and sg == 0:
                    row = lax.broadcasted_iota(jnp.int32, (HALF, HALF), 0)
                    col = lax.broadcasted_iota(jnp.int32, (HALF, HALF), 1)
                    v = jnp.where((row == col) & (core == 0), -v, v)
                loss = jnp.log(1.0 + jnp.exp2(v))
                u_scr[2 * su + hu] += loss
                g_scr[sg, hu] += jnp.sum(loss.reshape(HALF // 8, 8, HALF), axis=0)

    def cover(u_list, g_list):
        for hu in range(2):
            for g in range(0, len(g_list), 2):
                for u in range(0, len(u_list), 4):
                    block(hu, u_list[u : u + 4], g_list[g : g + 2])

    every = list(range(slots))
    cover(every[first_new:], every)
    if first_new:
        cover(every[:first_new], every[first_new:])
    u_out[...] = u_in[...]
    g_out[...] = g_in[...]
    for s in every:
        for hu in range(2):
            row = jnp.sum(u_scr[2 * s + hu].T, axis=0, keepdims=True)
            u_out[s : s + 1, hu * HALF : (hu + 1) * HALF] += row
            g_start = pl.multiple_of((core ^ hu) * HALF, HALF)
            g_out[s : s + 1, pl.ds(g_start, HALF)] += jnp.sum(g_scr[s, hu], axis=0, keepdims=True)


def tiles(us, gs, first_new, with_diag, ints, floats, u_acc, g_acc):
    sizes = tuple(u.shape[0] for u in us)
    slots = sum(sizes)
    pairs = slots * slots - first_new * first_new
    smem = pl.BlockSpec(memory_space=pltpu.SMEM)
    vmem = pl.BlockSpec(memory_space=pltpu.VMEM)
    acc = jax.ShapeDtypeStruct((RING, ROWS), jnp.float32)
    return pl.pallas_call(
        functools.partial(tile_kernel, sizes, first_new, with_diag),
        out_shape=(acc, acc),
        in_specs=[smem, smem] + [vmem] * (2 * len(us) + 2),
        out_specs=(vmem, vmem),
        scratch_shapes=[
            pltpu.VMEM((2 * slots, HALF, HALF), jnp.float32),
            pltpu.VMEM((slots, 2, 8, HALF), jnp.float32),
        ],
        compiler_params=pltpu.CompilerParams(vmem_limit_bytes=32 * 2**20),
        cost_estimate=pl.CostEstimate(
            flops=pairs * ROWS * ROWS * DEPTH,
            bytes_accessed=4 * slots * ROWS * DEPTH,
            transcendentals=pairs * ROWS * ROWS,
        ),
        name="tiles",
    )(ints, floats, *us, *gs, u_acc, g_acc)


def local(image_learner, image_reference, text_learner, text_reference):
    share = lax.axis_index("width")
    row = lax.axis_index("row")
    h, c = share // C, share % C
    y, z, x = row // (Z * X), row // X % Z, row % X
    spot = jnp.where(c == 0, z, jnp.where(y == 0, x, RING - 1 - x))
    at_zero, low = c == 0, h == 0

    il, ir, tl, tr = (a.T for a in (image_learner, image_reference, text_learner, text_reference))
    keep = jnp.where(at_zero, jnp.stack([il, ir]), jnp.stack([tl, tr]))
    away = jnp.where(at_zero, jnp.stack([tl, tr]), jnp.stack([il, ir]))
    got = send(away, CORES)
    both = jnp.concatenate(
        [jnp.where(at_zero, keep, got), jnp.where(at_zero, got, keep)], axis=1
    )
    p0 = jnp.where(low, both[0], both[1])
    q0 = send(jnp.where(low, both[1], both[0]), HALVES)

    ints = jnp.stack([c]).astype(jnp.int32)
    floats = jnp.where(
        low,
        jnp.array([40.0 * LOG2E, -2.0 * LOG2E], jnp.float32),
        jnp.array([20.0 * LOG2E, -1.0 * LOG2E], jnp.float32),
    )

    def step(pf, pb, qf, qb):
        return (send(pf, AHEAD), send(pb, BACK), send(qf, AHEAD), send(qb, BACK))

    u0 = prep([(p0, q0)])
    g0 = send(u0, CORES)
    us, gs = [u0], [g0]
    pf = pb = p0
    qf = qb = q0
    u_acc = g_acc = jnp.zeros((RING, ROWS), jnp.float32)
    for s in range(1, 4):
        pf, pb, qf, qb = step(pf, pb, qf, qb)
        u = prep([(pf, qf), (pb, qb)])
        us.append(u)
        gs.append(send(u, CORES))
        first = 0 if s == 1 else 2 * s - 1
        u_acc, g_acc = tiles(us, gs, first, s == 1, ints, floats, u_acc, g_acc)
    pf, pb, qf, qb = step(pf[:QUARTER], pb[QUARTER:], qf[:QUARTER], qb[QUARTER:])
    u = prep([(pf, pb, qf, qb)])
    us.append(u)
    gs.append(send(u, CORES))
    u_acc, g_acc = tiles(us, gs, 7, False, ints, floats, u_acc, g_acc)

    sums = u_acc + send(g_acc, CORES)
    sums = jnp.concatenate([sums[s : s + 1] for s in SLOT + SLOT], axis=0)
    sums = lax.dynamic_slice_in_dim(sums, RING - spot, RING, 0)
    sums = jnp.where(low, sums, -sums) * jnp.float32(1.0 / TOTAL)
    sums = lax.all_to_all(
        sums.reshape(2 * RING, HALF), AXES, 0, 0, axis_index_groups=GROUPS, tiled=True
    )
    sums = jnp.sum(sums, axis=0)
    mine = jnp.where(at_zero, sums[:64], sums[64:])
    other = send(jnp.where(at_zero, sums[64:], sums[:64]), CORES)
    return jnp.where(at_zero, mine, other), jnp.where(at_zero, other, mine)


def solution(mesh):
    spec = jax.sharding.PartitionSpec
    return jax.shard_map(
        local,
        mesh=mesh,
        in_specs=(spec("row", "width"),) * 4,
        out_specs=(spec(AXES),) * 2,
        check_vma=False,
    )
```

```python
import functools

import jax
import jax.numpy as jnp
import numpy as np
from jax import lax
from jax.experimental import pallas as pl
from jax.experimental.pallas import tpu as pltpu

AXES = ("row", "width")
Y, Z, X, H, C = 2, 8, 4, 2, 2
RING = 8
ROWS = 256
HALF = 128
DEPTH = 1152
QUARTER = 288
TOTAL = 16384
LOG2E = 1.4426950408889634
SLOT = (0, 2, 4, 6, 7, 5, 3, 1)


def device(y, z, x, h, c):
    return (((y * Z + z) * X + x) * H + h) * C + c


def place(p):
    p %= RING
    return (0, p) if p < X else (1, RING - 1 - p)


def route(d):
    pairs = []
    for y in range(Y):
        for z in range(Z):
            for x in range(X):
                ny, nx = place((x if y == 0 else RING - 1 - x) + d)
                for h in range(H):
                    pairs.append((device(y, z, x, h, 0), device(y, (z + d) % Z, x, h, 0)))
                    pairs.append((device(y, z, x, h, 1), device(ny, z, nx, h, 1)))
    return pairs


CORES = [(i, i ^ 1) for i in range(Y * Z * X * H * C)]
HALVES = [(i, i ^ 2) for i in range(Y * Z * X * H * C)]
AHEAD, BACK = route(1), route(-1)
GROUPS = [
    [device(y, z, x, h, 0) for z in range(Z) for h in range(H)] for y in range(Y) for x in range(X)
] + [
    [device(place(p)[0], z, place(p)[1], h, 1) for p in range(RING) for h in range(H)]
    for z in range(Z)
]


def send(x, route):
    return lax.ppermute(x, AXES, route)


def prep_kernel(n, *refs):
    ins, outs, scr = refs[: 2 * n], refs[2 * n : 3 * n], refs[3 * n]
    for b, out in enumerate(outs):
        parts = ins[2 * b : 2 * b + 2]
        acc = jnp.zeros((16, ROWS), jnp.float32)
        for part in parts:
            for r in range(0, part.shape[0], 16):
                v = part[r : r + 16, :].astype(jnp.float32)
                acc = acc + v * v
        inv = lax.rsqrt(jnp.sum(acc, axis=0, keepdims=True) + 1e-06)
        off = 0
        for part in parts:
            for r in range(0, part.shape[0], 16):
                v = part[r : r + 16, :].astype(jnp.float32)
                scr[off + r : off + r + 16, :] = (v * inv).astype(jnp.bfloat16)
            off += part.shape[0]
        for k in range(0, DEPTH, 128):
            out[:, k : k + 128] = scr[k : k + 128, :].T


def prep(*blocks):
    n = len(blocks)
    vmem = pl.BlockSpec(memory_space=pltpu.VMEM)
    return pl.pallas_call(
        functools.partial(prep_kernel, n),
        out_shape=[jax.ShapeDtypeStruct((ROWS, DEPTH), jnp.bfloat16)] * n,
        in_specs=[vmem] * (2 * n),
        out_specs=[vmem] * n,
        scratch_shapes=[pltpu.VMEM((DEPTH, ROWS), jnp.bfloat16)],
        compiler_params=pltpu.CompilerParams(vmem_limit_bytes=8 * 2**20),
        cost_estimate=pl.CostEstimate(
            flops=4 * n * ROWS * DEPTH, bytes_accessed=4 * n * ROWS * DEPTH, transcendentals=0
        ),
        name="prep",
    )(*[p for b in blocks for p in b])


def tile_kernel(news, olds, ins, *refs):
    refs = list(refs)

    def take(blocks):
        return [(slot, [refs.pop(0) for _ in range(n)]) for slot, n in blocks]

    new, old, in_u, in_g = take(news), take(olds), take(ins), take(ins)
    u_in, g_in, u_out, g_out, u_scr, g_scr = refs
    share = lax.axis_index("width")
    core, low = share % C, share < C
    scale = jnp.where(low, jnp.float32(40.0 * LOG2E), jnp.float32(20.0 * LOG2E))
    shift = jnp.where(low, jnp.float32(-2.0 * LOG2E), jnp.float32(-1.0 * LOG2E))
    u_scr[...] = jnp.zeros_like(u_scr)
    g_scr[...] = jnp.zeros_like(g_scr)
    u_slots = [slot for slot, _ in new + in_u]

    def whole(parts):
        values = [part[...] for part in parts]
        return values[0] if len(values) == 1 else jnp.concatenate(values, axis=0)

    def half(parts, k):
        return parts[k][...] if len(parts) == 2 else parts[0][k * HALF : (k + 1) * HALF, :]

    def losses(left, right, diag=False):
        v = lax.dot_general(
            left, right, (((1,), (1,)), ((), ())), preferred_element_type=jnp.float32
        )
        v = v * scale + shift
        if diag:
            row = lax.broadcasted_iota(jnp.int32, v.shape, 0)
            col = lax.broadcasted_iota(jnp.int32, v.shape, 1)
            v = jnp.where(row == col, -v, v)
        return jnp.log(1.0 + jnp.exp2(v))

    def rows(loss):
        return sum(loss[:, k : k + 128] for k in range(0, loss.shape[1], 128))

    def columns(loss):
        return jnp.sum(loss.reshape(loss.shape[0] // 8, 8, loss.shape[1]), axis=0)

    if new:
        left = jnp.concatenate([whole(parts) for _, parts in new], axis=0)
        for sg, parts in old:
            loss = losses(left, whole(parts))
            for i in range(len(new)):
                u_scr[i] += rows(loss[i * ROWS : (i + 1) * ROWS])
            g_scr[sg] += columns(loss)
    if len(ins) == 2:
        loss = losses(whole(in_u[0][1]), whole(in_g[1][1]))
        u_scr[len(new)] += rows(loss)
        g_scr[in_g[1][0]] += columns(loss)

    def own(flip):
        for i, (slot, parts) in enumerate(in_u):
            for k in range(2):
                m = k ^ flip
                loss = losses(half(parts, k), half(in_g[i][1], m), slot == 0 and flip == 0)
                u_scr[len(new) + i, k * HALF : (k + 1) * HALF, :] += loss
                g_scr[slot, :, m * HALF : (m + 1) * HALF] += columns(loss)

    if ins:
        pl.when(core == 0)(lambda: own(0))
        pl.when(core == 1)(lambda: own(1))
    u_out[...] = u_in[...]
    for i, slot in enumerate(u_slots):
        u_out[slot : slot + 1, :] += jnp.sum(u_scr[i].T, axis=0, keepdims=True)
    g_out[...] = g_in[...] + jnp.sum(g_scr[...], axis=1)


def tiles(news, olds, ins, acc):
    operands = [p for parts in news.values() for p in parts]
    operands += [p for parts in olds.values() for p in parts]
    for k in range(2):
        operands += [p for parts in ins.values() for p in parts[k]]
    shape = [
        tuple((slot, len(parts)) for slot, parts in news.items()),
        tuple((slot, len(parts)) for slot, parts in olds.items()),
        tuple((slot, len(parts[0])) for slot, parts in ins.items()),
    ]
    pairs = len(news) * len(olds) + len(ins) ** 2 / 2
    vmem = pl.BlockSpec(memory_space=pltpu.VMEM)
    sums = jax.ShapeDtypeStruct((RING, ROWS), jnp.float32)
    return pl.pallas_call(
        functools.partial(tile_kernel, *shape),
        out_shape=(sums, sums),
        in_specs=[vmem] * (len(operands) + 2),
        out_specs=(vmem, vmem),
        scratch_shapes=[
            pltpu.VMEM((len(news) + len(ins), ROWS, 128), jnp.float32),
            pltpu.VMEM((RING, 8, ROWS), jnp.float32),
        ],
        compiler_params=pltpu.CompilerParams(vmem_limit_bytes=12 * 2**20),
        cost_estimate=pl.CostEstimate(
            flops=int(pairs * 2 * ROWS * ROWS * DEPTH),
            bytes_accessed=2 * DEPTH * sum(o.shape[0] for o in operands),
            transcendentals=int(pairs * 2 * ROWS * ROWS),
        ),
        name="tiles",
    )(*operands, *acc)


def fold_kernel(mine, other, out):
    share, row = lax.axis_index("width"), lax.axis_index("row")
    y, z, x = row // (Z * X), row // X % Z, row % X
    spot = jnp.where(share % C == 0, z, jnp.where(y == 0, x, RING - 1 - x))
    scale = jnp.where(share < C, jnp.float32(1.0 / TOTAL), jnp.float32(-1.0 / TOTAL))
    for d, s in enumerate(SLOT):
        to = 2 * lax.rem(spot + d, RING)
        both = (mine[s : s + 1, :] + other[s : s + 1, :]) * scale
        for k in range(2):
            out[pl.ds(to + k, 1), :] = both[:, k * HALF : (k + 1) * HALF]


def fold(mine, other):
    vmem = pl.BlockSpec(memory_space=pltpu.VMEM)
    return pl.pallas_call(
        fold_kernel,
        out_shape=jax.ShapeDtypeStruct((2 * RING, HALF), jnp.float32),
        in_specs=[vmem, vmem],
        out_specs=vmem,
        compiler_params=pltpu.CompilerParams(vmem_limit_bytes=2**20),
        name="fold",
    )(mine, other)


def local(image_learner, image_reference, text_learner, text_reference):
    share = lax.axis_index("width")
    at_zero, low = share % C == 0, share < C

    il, ir, tl, tr = (a.T for a in (image_learner, image_reference, text_learner, text_reference))
    keep = jnp.where(at_zero, jnp.stack([il, ir]), jnp.stack([tl, tr]))
    away = jnp.where(at_zero, jnp.stack([tl, tr]), jnp.stack([il, ir]))
    got = send(away, CORES)
    both = jnp.concatenate(
        [jnp.where(at_zero, keep, got), jnp.where(at_zero, got, keep)], axis=1
    )
    p0 = jnp.where(low, both[0], both[1])
    q0 = send(jnp.where(low, both[1], both[0]), HALVES)

    def step(f, b):
        return send(f, AHEAD), send(b, BACK)

    tie = lax.optimization_barrier
    zero = jnp.zeros((RING, ROWS), jnp.float32)
    acc = (zero, zero)
    u, g = {}, {}

    def add(slot, *parts):
        u[slot] = parts
        g[slot] = tuple(send(p, CORES) for p in parts)

    def work(acc, new, ins):
        news = {s: u[s] for s in new}
        olds = {s: g[s] for s in range(min(new))} if new else {}
        return tiles(news, olds, {s: (u[s], g[s]) for s in ins}, acc)

    p1 = step(p0, p0)
    q1 = step(q0, q0)
    add(0, *prep((p0, q0)))
    f, b = prep((p1[0], q1[0]), (p1[1], q1[1]))
    for s in (1, 2):
        add(2 * s - 1, f)
        add(2 * s, b)
        f, b = step(f, b)
        acc = work(acc, (2 * s - 1, 2 * s), (0,) if s == 1 else (1, 2))
        f, b, acc = tie((f, b, acc))
    add(5, f)
    add(6, b)
    f, b = step(f[:HALF], b[HALF:])
    acc = work(acc, (5, 6), (3, 4))
    f, b, acc = tie((f, b, acc))
    add(7, f, b)
    acc = work(acc, (7,), (5, 6))
    u_acc, g_acc = work(acc, (), (7,))

    sums = fold(u_acc, send(g_acc, CORES))
    sums = lax.all_to_all(sums, AXES, 0, 0, axis_index_groups=GROUPS, tiled=True)
    sums = jnp.sum(sums, axis=0)
    mine = jnp.where(at_zero, sums[:64], sums[64:])
    other = send(jnp.where(at_zero, sums[64:], sums[:64]), CORES)
    return jnp.where(at_zero, mine, other), jnp.where(at_zero, other, mine)


def solution(mesh):
    spec = jax.sharding.PartitionSpec
    return jax.shard_map(
        local,
        mesh=mesh,
        in_specs=(spec("row", "width"),) * 4,
        out_specs=(spec(AXES),) * 2,
        check_vma=False,
    )
```

```python
import functools

import jax
import jax.numpy as jnp
import numpy as np
from jax import lax
from jax.experimental import pallas as pl
from jax.experimental.pallas import tpu as pltpu

AXES = ("row", "width")
Y, Z, X, H, C = 2, 8, 4, 2, 2
RING = 8
ROWS = 256
HALF = 128
DEPTH = 1152
QUARTER = 288
TOTAL = 16384
LOG2E = 1.4426950408889634
SLOT = (0, 2, 4, 6, 7, 5, 3, 1)


def device(y, z, x, h, c):
    return (((y * Z + z) * X + x) * H + h) * C + c


def place(p):
    p %= RING
    return (0, p) if p < X else (1, RING - 1 - p)


def route(d):
    pairs = []
    for y in range(Y):
        for z in range(Z):
            for x in range(X):
                ny, nx = place((x if y == 0 else RING - 1 - x) + d)
                for h in range(H):
                    pairs.append((device(y, z, x, h, 0), device(y, (z + d) % Z, x, h, 0)))
                    pairs.append((device(y, z, x, h, 1), device(ny, z, nx, h, 1)))
    return pairs


CORES = [(i, i ^ 1) for i in range(Y * Z * X * H * C)]
HALVES = [(i, i ^ 2) for i in range(Y * Z * X * H * C)]
AHEAD, BACK = route(1), route(-1)
GROUPS = [
    [device(y, z, x, h, 0) for z in range(Z) for h in range(H)] for y in range(Y) for x in range(X)
] + [
    [device(place(p)[0], z, place(p)[1], h, 1) for p in range(RING) for h in range(H)]
    for z in range(Z)
]


def send(x, route):
    return lax.ppermute(x, AXES, route)


def prep_kernel(n, *refs):
    ins, outs, scr = refs[: 2 * n], refs[2 * n : 3 * n], refs[3 * n]
    for b, out in enumerate(outs):
        parts = ins[2 * b : 2 * b + 2]
        acc = jnp.zeros((16, ROWS), jnp.float32)
        for part in parts:
            for r in range(0, part.shape[0], 16):
                v = part[r : r + 16, :].astype(jnp.float32)
                acc = acc + v * v
        inv = lax.rsqrt(jnp.sum(acc, axis=0, keepdims=True) + 1e-06)
        off = 0
        for part in parts:
            for r in range(0, part.shape[0], 16):
                v = part[r : r + 16, :].astype(jnp.float32)
                scr[off + r : off + r + 16, :] = (v * inv).astype(jnp.bfloat16)
            off += part.shape[0]
        for k in range(0, DEPTH, 128):
            out[:, k : k + 128] = scr[k : k + 128, :].T


def prep(*blocks):
    n = len(blocks)
    vmem = pl.BlockSpec(memory_space=pltpu.VMEM)
    return pl.pallas_call(
        functools.partial(prep_kernel, n),
        out_shape=[jax.ShapeDtypeStruct((ROWS, DEPTH), jnp.bfloat16)] * n,
        in_specs=[vmem] * (2 * n),
        out_specs=[vmem] * n,
        scratch_shapes=[pltpu.VMEM((DEPTH, ROWS), jnp.bfloat16)],
        compiler_params=pltpu.CompilerParams(vmem_limit_bytes=8 * 2**20),
        cost_estimate=pl.CostEstimate(
            flops=4 * n * ROWS * DEPTH, bytes_accessed=4 * n * ROWS * DEPTH, transcendentals=0
        ),
        name="prep",
    )(*[p for b in blocks for p in b])


def tile_kernel(news, olds, ins, *refs):
    refs = list(refs)

    def take(blocks):
        return [(slot, [refs.pop(0) for _ in range(n)]) for slot, n in blocks]

    new, old, in_u, in_g = take(news), take(olds), take(ins), take(ins)
    u_in, g_in, u_out, g_out, u_scr, g_scr = refs
    share = lax.axis_index("width")
    core, low = share % C, share < C
    scale = jnp.where(low, jnp.float32(40.0 * LOG2E), jnp.float32(20.0 * LOG2E))
    shift = jnp.where(low, jnp.float32(-2.0 * LOG2E), jnp.float32(-1.0 * LOG2E))
    u_scr[...] = jnp.zeros_like(u_scr)
    g_scr[...] = jnp.zeros_like(g_scr)
    u_slots = [slot for slot, _ in new + in_u]

    def whole(parts):
        values = [part[...] for part in parts]
        return values[0] if len(values) == 1 else jnp.concatenate(values, axis=0)

    def half(parts, k):
        return parts[k][...] if len(parts) == 2 else parts[0][k * HALF : (k + 1) * HALF, :]

    def losses(left, right, diag=False):
        v = lax.dot_general(
            left, right, (((1,), (1,)), ((), ())), preferred_element_type=jnp.float32
        )
        v = v * scale + shift
        if diag:
            row = lax.broadcasted_iota(jnp.int32, v.shape, 0)
            col = lax.broadcasted_iota(jnp.int32, v.shape, 1)
            v = jnp.where(row == col, -v, v)
        return jnp.log(1.0 + jnp.exp2(v))

    def rows(loss):
        return sum(loss[:, k : k + 128] for k in range(0, loss.shape[1], 128))

    def columns(loss):
        return jnp.sum(loss.reshape(loss.shape[0] // 8, 8, loss.shape[1]), axis=0)

    if new:
        left = jnp.concatenate([whole(parts) for _, parts in new], axis=0)
        for sg, parts in old:
            loss = losses(left, whole(parts))
            for i in range(len(new)):
                u_scr[i] += rows(loss[i * ROWS : (i + 1) * ROWS])
            g_scr[sg] += columns(loss)
    for j in range(len(ins)):
        for sg, parts in in_g[:j]:
            loss = losses(whole(in_u[j][1]), whole(parts))
            u_scr[len(new) + j] += rows(loss)
            g_scr[sg] += columns(loss)

    def own(flip):
        for i, (slot, parts) in enumerate(in_u):
            for k in range(2):
                m = k ^ flip
                loss = losses(half(parts, k), half(in_g[i][1], m), slot == 0 and flip == 0)
                u_scr[len(new) + i, k * HALF : (k + 1) * HALF, :] += loss
                g_scr[slot, :, m * HALF : (m + 1) * HALF] += columns(loss)

    if ins:
        pl.when(core == 0)(lambda: own(0))
        pl.when(core == 1)(lambda: own(1))
    u_out[...] = u_in[...]
    for i, slot in enumerate(u_slots):
        u_out[slot : slot + 1, :] += jnp.sum(u_scr[i].T, axis=0, keepdims=True)
    g_out[...] = g_in[...] + jnp.sum(g_scr[...], axis=1)


def tiles(news, olds, ins, acc):
    operands = [p for parts in news.values() for p in parts]
    operands += [p for parts in olds.values() for p in parts]
    for k in range(2):
        operands += [p for parts in ins.values() for p in parts[k]]
    shape = [
        tuple((slot, len(parts)) for slot, parts in news.items()),
        tuple((slot, len(parts)) for slot, parts in olds.items()),
        tuple((slot, len(parts[0])) for slot, parts in ins.items()),
    ]
    pairs = len(news) * len(olds) + len(ins) ** 2 / 2
    vmem = pl.BlockSpec(memory_space=pltpu.VMEM)
    sums = jax.ShapeDtypeStruct((RING, ROWS), jnp.float32)
    return pl.pallas_call(
        functools.partial(tile_kernel, *shape),
        out_shape=(sums, sums),
        in_specs=[vmem] * (len(operands) + 2),
        out_specs=(vmem, vmem),
        scratch_shapes=[
            pltpu.VMEM((len(news) + len(ins), ROWS, 128), jnp.float32),
            pltpu.VMEM((RING, 8, ROWS), jnp.float32),
        ],
        compiler_params=pltpu.CompilerParams(vmem_limit_bytes=12 * 2**20),
        cost_estimate=pl.CostEstimate(
            flops=int(pairs * 2 * ROWS * ROWS * DEPTH),
            bytes_accessed=2 * DEPTH * sum(o.shape[0] for o in operands),
            transcendentals=int(pairs * 2 * ROWS * ROWS),
        ),
        name="tiles",
    )(*operands, *acc)


def fold_kernel(mine, other, out):
    share, row = lax.axis_index("width"), lax.axis_index("row")
    y, z, x = row // (Z * X), row // X % Z, row % X
    spot = jnp.where(share % C == 0, z, jnp.where(y == 0, x, RING - 1 - x))
    scale = jnp.where(share < C, jnp.float32(1.0 / TOTAL), jnp.float32(-1.0 / TOTAL))
    for d, s in enumerate(SLOT):
        to = 2 * lax.rem(spot + d, RING)
        both = (mine[s : s + 1, :] + other[s : s + 1, :]) * scale
        for k in range(2):
            out[pl.ds(to + k, 1), :] = both[:, k * HALF : (k + 1) * HALF]


def fold(mine, other):
    vmem = pl.BlockSpec(memory_space=pltpu.VMEM)
    return pl.pallas_call(
        fold_kernel,
        out_shape=jax.ShapeDtypeStruct((2 * RING, HALF), jnp.float32),
        in_specs=[vmem, vmem],
        out_specs=vmem,
        compiler_params=pltpu.CompilerParams(vmem_limit_bytes=2**20),
        name="fold",
    )(mine, other)


def local(image_learner, image_reference, text_learner, text_reference):
    share = lax.axis_index("width")
    at_zero, low = share % C == 0, share < C

    il, ir, tl, tr = (a.T for a in (image_learner, image_reference, text_learner, text_reference))
    keep = jnp.where(at_zero, jnp.stack([il, ir]), jnp.stack([tl, tr]))
    away = jnp.where(at_zero, jnp.stack([tl, tr]), jnp.stack([il, ir]))
    keep, away = lax.optimization_barrier((keep, away))
    got = send(away, CORES)
    both = jnp.concatenate(
        [jnp.where(at_zero, keep, got), jnp.where(at_zero, got, keep)], axis=1
    )
    p0 = jnp.where(low, both[0], both[1])
    q0 = send(jnp.where(low, both[1], both[0]), HALVES)

    def step(f, b):
        return send(f, AHEAD), send(b, BACK)

    tie = lax.optimization_barrier
    zero = jnp.zeros((RING, ROWS), jnp.float32)
    acc = (zero, zero)
    u, g = {}, {}

    def add(slot, *parts):
        u[slot] = parts
        g[slot] = tuple(send(p, CORES) for p in parts)

    def work(acc, new, ins):
        news = {s: u[s] for s in new}
        olds = {s: g[s] for s in range(min(new))} if new else {}
        return tiles(news, olds, {s: (u[s], g[s]) for s in ins}, acc)

    p1 = step(p0, p0)
    q0, p1 = tie((q0, p1))
    q1 = step(q0, q0)
    p2 = step(*p1)
    q2 = step(*q1)
    f, b = prep((p2[0], q2[0]), (p2[1], q2[1]))
    f, b, p0, p1, q0, q1 = tie((f, b, p0, p1, q0, q1))
    add(3, f)
    add(4, b)
    f, b = step(f, b)
    first = prep((p0, q0), (p1[0], q1[0]), (p1[1], q1[1]))
    for s in range(3):
        add(s, first[s])
    acc = work(acc, (3, 4), (0, 1, 2))
    f, b, acc = tie((f, b, acc))
    add(5, f)
    add(6, b)
    f, b = step(f[:HALF], b[HALF:])
    acc = work(acc, (5, 6), (3, 4))
    acc = work(acc, (), (5, 6))
    f, b, acc = tie((f, b, acc))
    add(7, f, b)
    acc = work(acc, (7,), ())
    u_acc, g_acc = work(acc, (), (7,))

    sums = fold(u_acc, send(g_acc, CORES))
    sums = lax.all_to_all(sums, AXES, 0, 0, axis_index_groups=GROUPS, tiled=True)
    sums = jnp.sum(sums, axis=0)
    mine = jnp.where(at_zero, sums[:64], sums[64:])
    other = send(jnp.where(at_zero, sums[64:], sums[:64]), CORES)
    return jnp.where(at_zero, mine, other), jnp.where(at_zero, other, mine)


def solution(mesh):
    spec = jax.sharding.PartitionSpec
    return jax.shard_map(
        local,
        mesh=mesh,
        in_specs=(spec("row", "width"),) * 4,
        out_specs=(spec(AXES),) * 2,
        check_vma=False,
    )
```

```python
import functools

import jax
import jax.numpy as jnp
import numpy as np
from jax import lax
from jax.experimental import pallas as pl
from jax.experimental.pallas import tpu as pltpu

AXES = ("row", "width")
Y, Z, X, H, C = 2, 8, 4, 2, 2
RING = 8
ROWS = 256
HALF = 128
DEPTH = 1152
QUARTER = 288
TOTAL = 16384
LOG2E = 1.4426950408889634
SLOT = (0, 2, 4, 6, 7, 5, 3, 1)


def device(y, z, x, h, c):
    return (((y * Z + z) * X + x) * H + h) * C + c


def place(p):
    p %= RING
    return (0, p) if p < X else (1, RING - 1 - p)


def route(d):
    pairs = []
    for y in range(Y):
        for z in range(Z):
            for x in range(X):
                ny, nx = place((x if y == 0 else RING - 1 - x) + d)
                for h in range(H):
                    pairs.append((device(y, z, x, h, 0), device(y, (z + d) % Z, x, h, 0)))
                    pairs.append((device(y, z, x, h, 1), device(ny, z, nx, h, 1)))
    return pairs


CORES = [(i, i ^ 1) for i in range(Y * Z * X * H * C)]
HALVES = [(i, i ^ 2) for i in range(Y * Z * X * H * C)]
AHEAD, BACK = route(1), route(-1)
GROUPS = [
    [device(y, z, x, h, 0) for z in range(Z) for h in range(H)] for y in range(Y) for x in range(X)
] + [
    [device(place(p)[0], z, place(p)[1], h, 1) for p in range(RING) for h in range(H)]
    for z in range(Z)
]


def send(x, route):
    return lax.ppermute(x, AXES, route)


def prep_kernel(n, *refs):
    ins, out, scr = refs[:-2], refs[-2], refs[-1]
    for b in range(n):
        parts = ins[2 * b : 2 * b + 2]
        acc = jnp.zeros((16, ROWS), jnp.float32)
        for part in parts:
            for r in range(0, part.shape[0], 16):
                v = part[r : r + 16, :].astype(jnp.float32)
                acc = acc + v * v
        inv = lax.rsqrt(jnp.sum(acc, axis=0, keepdims=True) + 1e-06)
        off = 0
        for part in parts:
            for r in range(0, part.shape[0], 16):
                v = part[r : r + 16, :].astype(jnp.float32)
                scr[off + r : off + r + 16, :] = (v * inv).astype(jnp.bfloat16)
            off += part.shape[0]
        for k in range(0, DEPTH, 128):
            out[b * ROWS : (b + 1) * ROWS, k : k + 128] = scr[k : k + 128, :].T


def prep(*blocks):
    n = len(blocks)
    vmem = pl.BlockSpec(memory_space=pltpu.VMEM)
    return pl.pallas_call(
        functools.partial(prep_kernel, n),
        out_shape=jax.ShapeDtypeStruct((n * ROWS, DEPTH), jnp.bfloat16),
        in_specs=[vmem] * (2 * n),
        out_specs=vmem,
        scratch_shapes=[pltpu.VMEM((DEPTH, ROWS), jnp.bfloat16)],
        compiler_params=pltpu.CompilerParams(vmem_limit_bytes=8 * 2**20),
        cost_estimate=pl.CostEstimate(
            flops=4 * n * ROWS * DEPTH, bytes_accessed=4 * n * ROWS * DEPTH, transcendentals=0
        ),
        name="prep",
    )(*[p for b in blocks for p in b])


def tile_kernel(where, news, olds, ins, *refs):
    u_in, g_in, u_out, g_out, u_scr, g_scr = refs[-6:]
    share = lax.axis_index("width")
    core, low = share % C, share < C
    scale = jnp.where(low, jnp.float32(40.0 * LOG2E), jnp.float32(20.0 * LOG2E))
    shift = jnp.where(low, jnp.float32(-2.0 * LOG2E), jnp.float32(-1.0 * LOG2E))
    u_scr[...] = jnp.zeros_like(u_scr)
    g_scr[...] = jnp.zeros_like(g_scr)
    u_slots = news + ins

    def block(side, slot, first=0, rows=ROWS):
        a, start = where[side][slot]
        return refs[a][start + first : start + first + rows, :]

    def losses(left, right, diag=False):
        v = lax.dot_general(
            left, right, (((1,), (1,)), ((), ())), preferred_element_type=jnp.float32
        )
        v = v * scale + shift
        if diag:
            row = lax.broadcasted_iota(jnp.int32, v.shape, 0)
            col = lax.broadcasted_iota(jnp.int32, v.shape, 1)
            v = jnp.where(row == col, -v, v)
        return jnp.log(1.0 + jnp.exp2(v))

    def rows(loss):
        return sum(loss[:, k : k + 128] for k in range(0, loss.shape[1], 128))

    def columns(loss):
        return jnp.sum(loss.reshape(loss.shape[0] // 8, 8, loss.shape[1]), axis=0)

    if news:
        left = jnp.concatenate([block(0, s) for s in news], axis=0)
        for sg in olds:
            loss = losses(left, block(1, sg))
            for i in range(len(news)):
                u_scr[i] += rows(loss[i * ROWS : (i + 1) * ROWS])
            g_scr[sg] += columns(loss)
    for j, su in enumerate(ins):
        for sg in ins[:j]:
            loss = losses(block(0, su), block(1, sg))
            u_scr[len(news) + j] += rows(loss)
            g_scr[sg] += columns(loss)

    def own(flip):
        for i, slot in enumerate(ins):
            for k in range(2):
                u, g = k * HALF, (k ^ flip) * HALF
                loss = losses(
                    block(0, slot, u, HALF), block(1, slot, g, HALF), slot == 0 and flip == 0
                )
                u_scr[len(news) + i, u : u + HALF, :] += loss
                g_scr[slot, :, g : g + HALF] += columns(loss)

    if ins:
        pl.when(core == 0)(lambda: own(0))
        pl.when(core == 1)(lambda: own(1))
    u_out[...] = u_in[...]
    for i, slot in enumerate(u_slots):
        u_out[slot : slot + 1, :] += jnp.sum(u_scr[i].T, axis=0, keepdims=True)
    g_out[...] = g_in[...] + jnp.sum(g_scr[...], axis=1)


def tiles(where, us, gs, news, olds, ins, acc):
    pairs = len(news) * len(olds) + len(ins) ** 2 / 2
    operands, sides = [], []
    for arrays, slots in ((us, news + ins), (gs, olds + ins)):
        used = sorted({where[s][0] for s in slots})
        sides.append({s: (len(operands) + used.index(where[s][0]), where[s][1]) for s in slots})
        operands += [arrays[a] for a in used]
    vmem = pl.BlockSpec(memory_space=pltpu.VMEM)
    sums = jax.ShapeDtypeStruct((RING, ROWS), jnp.float32)
    return pl.pallas_call(
        functools.partial(tile_kernel, sides, news, olds, ins),
        out_shape=(sums, sums),
        in_specs=[vmem] * (len(operands) + 2),
        out_specs=(vmem, vmem),
        scratch_shapes=[
            pltpu.VMEM((len(news) + len(ins), ROWS, 128), jnp.float32),
            pltpu.VMEM((RING, 8, ROWS), jnp.float32),
        ],
        compiler_params=pltpu.CompilerParams(vmem_limit_bytes=16 * 2**20),
        cost_estimate=pl.CostEstimate(
            flops=int(pairs * 2 * ROWS * ROWS * DEPTH),
            bytes_accessed=2 * DEPTH * sum(o.shape[0] for o in operands),
            transcendentals=int(pairs * 2 * ROWS * ROWS),
        ),
        name="tiles",
    )(*operands, *acc)


def fold_kernel(mine, other, out):
    share, row = lax.axis_index("width"), lax.axis_index("row")
    y, z, x = row // (Z * X), row // X % Z, row % X
    spot = jnp.where(share % C == 0, z, jnp.where(y == 0, x, RING - 1 - x))
    scale = jnp.where(share < C, jnp.float32(1.0 / TOTAL), jnp.float32(-1.0 / TOTAL))
    for d, s in enumerate(SLOT):
        to = 2 * lax.rem(spot + d, RING)
        both = (mine[s : s + 1, :] + other[s : s + 1, :]) * scale
        for k in range(2):
            out[pl.ds(to + k, 1), :] = both[:, k * HALF : (k + 1) * HALF]


def fold(mine, other):
    vmem = pl.BlockSpec(memory_space=pltpu.VMEM)
    return pl.pallas_call(
        fold_kernel,
        out_shape=jax.ShapeDtypeStruct((2 * RING, HALF), jnp.float32),
        in_specs=[vmem, vmem],
        out_specs=vmem,
        compiler_params=pltpu.CompilerParams(vmem_limit_bytes=2**20),
        name="fold",
    )(mine, other)


def local(image_learner, image_reference, text_learner, text_reference):
    share = lax.axis_index("width")
    at_zero, low = share % C == 0, share < C

    il, ir, tl, tr = (a.T for a in (image_learner, image_reference, text_learner, text_reference))

    def pick(own_type, own_kind):
        image, text = (jnp.where(low == own_type, l, r) for l, r in ((il, ir), (tl, tr)))
        return jnp.where(at_zero == own_kind, image, text)

    tie = lax.optimization_barrier
    mine, p_away, q_away = tie(
        (pick(True, True), pick(True, False), jnp.stack([pick(False, True), pick(False, False)]))
    )

    def in_order(same, cross):
        return jnp.where(
            at_zero, jnp.concatenate([same, cross], 0), jnp.concatenate([cross, same], 0)
        )

    p0 = in_order(mine, send(p_away, CORES))
    q_same, q_cross = send(q_away, HALVES)
    q0 = in_order(q_same, send(q_cross, CORES))

    def step(f, b):
        b = send(b, BACK)
        return send(f, AHEAD), b

    zero = jnp.zeros((RING, ROWS), jnp.float32)
    acc = (zero, zero)
    us, gs, where = [], [], {}

    def add(slots, *blocks):
        u = prep(*blocks)
        for i, slot in enumerate(slots):
            where[slot] = (len(us), i * ROWS)
        us.append(u)
        gs.append(send(u, CORES))

    def work(acc, news, olds, ins):
        return tiles(where, us, gs, news, olds, ins, acc)

    p1 = step(p0, p0)
    q0, p1 = tie((q0, p1))
    q1 = step(q0, q0)
    p2 = step(*p1)
    q2 = step(*q1)
    p3 = step(*p2)
    q3 = step(*q2)
    p4 = send(p3[0], AHEAD)
    q4 = send(q3[1], BACK)
    p3, q3, p0, p1, p2, q0, q1, q2 = tie((p3, q3, p0, p1, p2, q0, q1, q2))
    add((0, 1, 2), (p0, q0), (p1[0], q1[0]), (p1[1], q1[1]))
    add((3, 4), (p2[0], q2[0]), (p2[1], q2[1]))
    acc = work(acc, (3, 4), (0, 1, 2), (0, 1, 2))
    add((5, 6), (p3[0], q3[0]), (p3[1], q3[1]))
    acc = work(acc, (5, 6), (0, 1, 2, 3, 4), (3, 4))
    p4, q4, acc = tie((p4, q4, acc))
    add((7,), (p4, q4))
    acc = work(acc, (7,), (0, 1, 2, 3, 4, 5, 6), (5, 6))
    u_acc, g_acc = work(acc, (), (), (7,))

    sums = fold(u_acc, send(g_acc, CORES))
    sums = lax.all_to_all(sums, AXES, 0, 0, axis_index_groups=GROUPS, tiled=True)
    sums = jnp.sum(sums, axis=0)
    mine = jnp.where(at_zero, sums[:64], sums[64:])
    other = send(jnp.where(at_zero, sums[64:], sums[:64]), CORES)
    return jnp.where(at_zero, mine, other), jnp.where(at_zero, other, mine)


def solution(mesh):
    spec = jax.sharding.PartitionSpec
    return jax.shard_map(
        local,
        mesh=mesh,
        in_specs=(spec("row", "width"),) * 4,
        out_specs=(spec(AXES),) * 2,
        check_vma=False,
    )
```

```python
import functools

import jax
import jax.numpy as jnp
import numpy as np
from jax import lax
from jax.experimental import pallas as pl
from jax.experimental.pallas import tpu as pltpu

AXES = ("row", "width")
Y, Z, X, H, C = 2, 8, 4, 2, 2
RING = 8
ROWS = 256
HALF = 128
DEPTH = 1152
QUARTER = 288
TOTAL = 16384
LOG2E = 1.4426950408889634
SLOT = (0, 2, 4, 6, 7, 5, 3, 1)


def device(y, z, x, h, c):
    return (((y * Z + z) * X + x) * H + h) * C + c


def place(p):
    p %= RING
    return (0, p) if p < X else (1, RING - 1 - p)


def route(d):
    pairs = []
    for y in range(Y):
        for z in range(Z):
            for x in range(X):
                ny, nx = place((x if y == 0 else RING - 1 - x) + d)
                for h in range(H):
                    pairs.append((device(y, z, x, h, 0), device(y, (z + d) % Z, x, h, 0)))
                    pairs.append((device(y, z, x, h, 1), device(ny, z, nx, h, 1)))
    return pairs


CORES = [(i, i ^ 1) for i in range(Y * Z * X * H * C)]
HALVES = [(i, i ^ 2) for i in range(Y * Z * X * H * C)]
AHEAD, BACK = route(1), route(-1)
GROUPS = [
    [device(y, z, x, h, 0) for z in range(Z) for h in range(H)] for y in range(Y) for x in range(X)
] + [
    [device(place(p)[0], z, place(p)[1], h, 1) for p in range(RING) for h in range(H)]
    for z in range(Z)
]


def send(x, route):
    return lax.ppermute(x, AXES, route)


def prep_kernel(n, *refs):
    ins, out, scr = refs[:-2], refs[-2], refs[-1]
    for b in range(n):
        parts = ins[2 * b : 2 * b + 2]
        acc = jnp.zeros((16, ROWS), jnp.float32)
        for part in parts:
            for r in range(0, part.shape[0], 16):
                v = part[r : r + 16, :].astype(jnp.float32)
                acc = acc + v * v
        inv = lax.rsqrt(jnp.sum(acc, axis=0, keepdims=True) + 1e-06)
        off = 0
        for part in parts:
            for r in range(0, part.shape[0], 16):
                v = part[r : r + 16, :].astype(jnp.float32)
                scr[off + r : off + r + 16, :] = (v * inv).astype(jnp.bfloat16)
            off += part.shape[0]
        for k in range(0, DEPTH, 128):
            out[b * ROWS : (b + 1) * ROWS, k : k + 128] = scr[k : k + 128, :].T


def prep(*blocks):
    n = len(blocks)
    vmem = pl.BlockSpec(memory_space=pltpu.VMEM)
    return pl.pallas_call(
        functools.partial(prep_kernel, n),
        out_shape=jax.ShapeDtypeStruct((n * ROWS, DEPTH), jnp.bfloat16),
        in_specs=[vmem] * (2 * n),
        out_specs=vmem,
        scratch_shapes=[pltpu.VMEM((DEPTH, ROWS), jnp.bfloat16)],
        compiler_params=pltpu.CompilerParams(vmem_limit_bytes=8 * 2**20),
        cost_estimate=pl.CostEstimate(
            flops=4 * n * ROWS * DEPTH, bytes_accessed=4 * n * ROWS * DEPTH, transcendentals=0
        ),
        name="prep",
    )(*[p for b in blocks for p in b])


def tile_kernel(where, news, olds, ins, *refs):
    u_in, g_in, u_out, g_out, u_scr, g_scr = refs[-6:]
    share = lax.axis_index("width")
    core, low = share % C, share < C
    scale = jnp.where(low, jnp.float32(40.0 * LOG2E), jnp.float32(20.0 * LOG2E))
    shift = jnp.where(low, jnp.float32(-2.0 * LOG2E), jnp.float32(-1.0 * LOG2E))
    u_slots, g_slots = news + ins, tuple(sorted(set(olds + ins)))
    u_scr[...] = jnp.zeros_like(u_scr)
    for slot in g_slots:
        g_scr[slot] = jnp.zeros_like(g_scr[slot])

    def block(side, slot, first=0, rows=ROWS):
        a, start = where[side][slot]
        return refs[a][start + first : start + first + rows, :]

    def losses(left, right, diag=False):
        v = lax.dot_general(
            left, right, (((1,), (1,)), ((), ())), preferred_element_type=jnp.float32
        )
        v = v * scale + shift
        if diag:
            row = lax.broadcasted_iota(jnp.int32, v.shape, 0)
            col = lax.broadcasted_iota(jnp.int32, v.shape, 1)
            v = jnp.where(row == col, -v, v)
        return jnp.log(1.0 + jnp.exp2(v))

    def rows(loss):
        return sum(loss[:, k : k + 128] for k in range(0, loss.shape[1], 128))

    def columns(loss):
        return jnp.sum(loss.reshape(loss.shape[0] // 8, 8, loss.shape[1]), axis=0)

    if news:
        left = jnp.concatenate([block(0, s) for s in news], axis=0)
        for sg in olds:
            loss = losses(left, block(1, sg))
            for i in range(len(news)):
                u_scr[i] += rows(loss[i * ROWS : (i + 1) * ROWS])
            g_scr[sg] += columns(loss)
    for j, su in enumerate(ins):
        for sg in ins[:j]:
            loss = losses(block(0, su), block(1, sg))
            u_scr[len(news) + j] += rows(loss)
            g_scr[sg] += columns(loss)

    def own(flip):
        for i, slot in enumerate(ins):
            for k in range(2):
                u, g = k * HALF, (k ^ flip) * HALF
                loss = losses(
                    block(0, slot, u, HALF), block(1, slot, g, HALF), slot == 0 and flip == 0
                )
                u_scr[len(news) + i, u : u + HALF, :] += loss
                g_scr[slot, :, g : g + HALF] += columns(loss)

    if ins:
        pl.when(core == 0)(lambda: own(0))
        pl.when(core == 1)(lambda: own(1))
    u_out[...] = u_in[...]
    for i, slot in enumerate(u_slots):
        u_out[slot : slot + 1, :] += jnp.sum(u_scr[i].T, axis=0, keepdims=True)
    g_out[...] = g_in[...]
    for slot in g_slots:
        g_out[slot : slot + 1, :] += jnp.sum(g_scr[slot], axis=0, keepdims=True)


def tiles(where, us, gs, news, olds, ins, acc):
    pairs = len(news) * len(olds) + len(ins) ** 2 / 2
    operands, sides = [], []
    for arrays, slots in ((us, news + ins), (gs, olds + ins)):
        used = sorted({where[s][0] for s in slots})
        sides.append({s: (len(operands) + used.index(where[s][0]), where[s][1]) for s in slots})
        operands += [arrays[a] for a in used]
    vmem = pl.BlockSpec(memory_space=pltpu.VMEM)
    sums = jax.ShapeDtypeStruct((RING, ROWS), jnp.float32)
    return pl.pallas_call(
        functools.partial(tile_kernel, sides, news, olds, ins),
        out_shape=(sums, sums),
        in_specs=[vmem] * (len(operands) + 2),
        out_specs=(vmem, vmem),
        scratch_shapes=[
            pltpu.VMEM((len(news) + len(ins), ROWS, 128), jnp.float32),
            pltpu.VMEM((RING, 8, ROWS), jnp.float32),
        ],
        compiler_params=pltpu.CompilerParams(vmem_limit_bytes=16 * 2**20),
        cost_estimate=pl.CostEstimate(
            flops=int(pairs * 2 * ROWS * ROWS * DEPTH),
            bytes_accessed=2 * DEPTH * sum(o.shape[0] for o in operands),
            transcendentals=int(pairs * 2 * ROWS * ROWS),
        ),
        name="tiles",
    )(*operands, *acc)


def fold_kernel(mine, other, out):
    share, row = lax.axis_index("width"), lax.axis_index("row")
    y, z, x = row // (Z * X), row // X % Z, row % X
    spot = jnp.where(share % C == 0, z, jnp.where(y == 0, x, RING - 1 - x))
    scale = jnp.where(share < C, jnp.float32(1.0 / TOTAL), jnp.float32(-1.0 / TOTAL))
    for d, s in enumerate(SLOT):
        to = 2 * lax.rem(spot + d, RING)
        both = (mine[s : s + 1, :] + other[s : s + 1, :]) * scale
        for k in range(2):
            out[pl.ds(to + k, 1), :] = both[:, k * HALF : (k + 1) * HALF]


def fold(mine, other):
    vmem = pl.BlockSpec(memory_space=pltpu.VMEM)
    return pl.pallas_call(
        fold_kernel,
        out_shape=jax.ShapeDtypeStruct((2 * RING, HALF), jnp.float32),
        in_specs=[vmem, vmem],
        out_specs=vmem,
        compiler_params=pltpu.CompilerParams(vmem_limit_bytes=2**20),
        name="fold",
    )(mine, other)


def local(image_learner, image_reference, text_learner, text_reference):
    share = lax.axis_index("width")
    at_zero, low = share % C == 0, share < C

    il, ir, tl, tr = (a.T for a in (image_learner, image_reference, text_learner, text_reference))

    def pick(own_type, own_kind):
        image, text = (jnp.where(low == own_type, l, r) for l, r in ((il, ir), (tl, tr)))
        return jnp.where(at_zero == own_kind, image, text)

    tie = lax.optimization_barrier
    mine, p_away, q_away = tie(
        (pick(True, True), pick(True, False), jnp.stack([pick(False, True), pick(False, False)]))
    )

    def in_order(same, cross):
        return jnp.where(
            at_zero, jnp.concatenate([same, cross], 0), jnp.concatenate([cross, same], 0)
        )

    p0 = in_order(mine, send(p_away, CORES))
    q_same, q_cross = send(q_away, HALVES)
    q0 = in_order(q_same, send(q_cross, CORES))

    def step(f, b):
        b = send(b, BACK)
        return send(f, AHEAD), b

    zero = jnp.zeros((RING, ROWS), jnp.float32)
    acc = (zero, zero)
    us, gs, where = [], [], {}

    def add(slots, *blocks):
        u = prep(*blocks)
        for i, slot in enumerate(slots):
            where[slot] = (len(us), i * ROWS)
        us.append(u)
        gs.append(send(u, CORES))

    def work(acc, news, olds, ins):
        return tiles(where, us, gs, news, olds, ins, acc)

    p1 = step(p0, p0)
    q0, p1 = tie((q0, p1))
    q1 = step(q0, q0)
    p2 = step(*p1)
    q2 = step(*q1)
    p3 = step(*p2)
    q3 = step(*q2)
    p4 = send(p3[0], AHEAD)
    q4 = send(q3[1], BACK)
    p3, q3, p0, p1, p2, q0, q1, q2 = tie((p3, q3, p0, p1, p2, q0, q1, q2))
    add((0, 1, 2), (p0, q0), (p1[0], q1[0]), (p1[1], q1[1]))
    add((3, 4), (p2[0], q2[0]), (p2[1], q2[1]))
    acc = work(acc, (3, 4), (0, 1, 2), (0, 1, 2))
    add((5, 6), (p3[0], q3[0]), (p3[1], q3[1]))
    acc = work(acc, (5, 6), (0, 1, 2, 3, 4), (3, 4))
    p4, q4, acc = tie((p4, q4, acc))
    add((7,), (p4, q4))
    acc = work(acc, (7,), (0, 1, 2, 3, 4, 5, 6), (5, 6))
    u_acc, g_acc = work(acc, (), (), (7,))

    sums = fold(u_acc, send(g_acc, CORES))
    sums = lax.all_to_all(sums, AXES, 0, 0, axis_index_groups=GROUPS, tiled=True)
    sums = jnp.sum(sums, axis=0)
    mine = jnp.where(at_zero, sums[:64], sums[64:])
    other = send(jnp.where(at_zero, sums[64:], sums[:64]), CORES)
    return jnp.where(at_zero, mine, other), jnp.where(at_zero, other, mine)


def solution(mesh):
    spec = jax.sharding.PartitionSpec
    return jax.shard_map(
        local,
        mesh=mesh,
        in_specs=(spec("row", "width"),) * 4,
        out_specs=(spec(AXES),) * 2,
        check_vma=False,
    )
```

```python
import functools

import jax
import jax.numpy as jnp
import numpy as np
from jax import lax
from jax.experimental import pallas as pl
from jax.experimental.pallas import tpu as pltpu

AXES = ("row", "width")
Y, Z, X, H, C = 2, 8, 4, 2, 2
RING = 8
ROWS = 256
HALF = 128
DEPTH = 1152
QUARTER = 288
TOTAL = 16384
LOG2E = 1.4426950408889634
SLOT = (0, 2, 4, 6, 7, 5, 3, 1)


def device(y, z, x, h, c):
    return (((y * Z + z) * X + x) * H + h) * C + c


def place(p):
    p %= RING
    return (0, p) if p < X else (1, RING - 1 - p)


def route(d):
    pairs = []
    for y in range(Y):
        for z in range(Z):
            for x in range(X):
                ny, nx = place((x if y == 0 else RING - 1 - x) + d)
                for h in range(H):
                    pairs.append((device(y, z, x, h, 0), device(y, (z + d) % Z, x, h, 0)))
                    pairs.append((device(y, z, x, h, 1), device(ny, z, nx, h, 1)))
    return pairs


CORES = [(i, i ^ 1) for i in range(Y * Z * X * H * C)]
HALVES = [(i, i ^ 2) for i in range(Y * Z * X * H * C)]
AHEAD, BACK = route(1), route(-1)
GROUPS = [
    [device(y, z, x, h, 0) for z in range(Z) for h in range(H)] for y in range(Y) for x in range(X)
] + [
    [device(place(p)[0], z, place(p)[1], h, 1) for p in range(RING) for h in range(H)]
    for z in range(Z)
]


def send(x, route):
    return lax.ppermute(x, AXES, route)


def prep_kernel(n, *refs):
    ins, out, scr = refs[:-2], refs[-2], refs[-1]
    for b in range(n):
        parts = ins[2 * b : 2 * b + 2]
        acc = jnp.zeros((16, ROWS), jnp.float32)
        for part in parts:
            for r in range(0, part.shape[0], 16):
                v = part[r : r + 16, :].astype(jnp.float32)
                acc = acc + v * v
        inv = lax.rsqrt(jnp.sum(acc, axis=0, keepdims=True) + 1e-06)
        off = 0
        for part in parts:
            for r in range(0, part.shape[0], 16):
                v = part[r : r + 16, :].astype(jnp.float32)
                scr[off + r : off + r + 16, :] = (v * inv).astype(jnp.bfloat16)
            off += part.shape[0]
        for k in range(0, DEPTH, 128):
            out[b * ROWS : (b + 1) * ROWS, k : k + 128] = scr[k : k + 128, :].T


def prep(*blocks):
    n = len(blocks)
    vmem = pl.BlockSpec(memory_space=pltpu.VMEM)
    return pl.pallas_call(
        functools.partial(prep_kernel, n),
        out_shape=jax.ShapeDtypeStruct((n * ROWS, DEPTH), jnp.bfloat16),
        in_specs=[vmem] * (2 * n),
        out_specs=vmem,
        scratch_shapes=[pltpu.VMEM((DEPTH, ROWS), jnp.bfloat16)],
        compiler_params=pltpu.CompilerParams(vmem_limit_bytes=8 * 2**20),
        cost_estimate=pl.CostEstimate(
            flops=4 * n * ROWS * DEPTH, bytes_accessed=4 * n * ROWS * DEPTH, transcendentals=0
        ),
        name="prep",
    )(*[p for b in blocks for p in b])


def tile_kernel(where, news, olds, ins, *refs):
    u_in, g_in, u_out, g_out, u_scr, g_scr = refs[-6:]
    share = lax.axis_index("width")
    core, low = share % C, share < C
    scale = jnp.where(low, jnp.float32(40.0 * LOG2E), jnp.float32(20.0 * LOG2E))
    shift = jnp.where(low, jnp.float32(-2.0 * LOG2E), jnp.float32(-1.0 * LOG2E))
    u_slots, g_slots = news + ins, tuple(sorted(set(olds + ins)))
    u_scr[...] = jnp.zeros_like(u_scr)
    for slot in g_slots:
        g_scr[slot] = jnp.zeros_like(g_scr[slot])

    def block(side, slot, first=0, rows=ROWS):
        a, start = where[side][slot]
        return refs[a][start + first : start + first + rows, :]

    def losses(left, right, diag=False):
        v = lax.dot_general(
            left, right, (((1,), (1,)), ((), ())), preferred_element_type=jnp.float32
        )
        v = v * scale + shift
        if diag:
            row = lax.broadcasted_iota(jnp.int32, v.shape, 0)
            col = lax.broadcasted_iota(jnp.int32, v.shape, 1)
            v = jnp.where(row == col, -v, v)
        return jnp.log(1.0 + jnp.exp2(v))

    def rows(loss):
        return sum(loss[:, k : k + 128] for k in range(0, loss.shape[1], 128))

    def columns(loss):
        return jnp.sum(loss.reshape(loss.shape[0] // 8, 8, loss.shape[1]), axis=0)

    if news:
        left = jnp.concatenate([block(0, s) for s in news], axis=0)
        for sg in olds:
            loss = losses(left, block(1, sg))
            for i in range(len(news)):
                u_scr[i] += rows(loss[i * ROWS : (i + 1) * ROWS])
            g_scr[sg] += columns(loss)
    for j, su in enumerate(ins):
        for sg in ins[:j]:
            loss = losses(block(0, su), block(1, sg))
            u_scr[len(news) + j] += rows(loss)
            g_scr[sg] += columns(loss)

    def own(flip):
        for i, slot in enumerate(ins):
            for k in range(2):
                u, g = k * HALF, (k ^ flip) * HALF
                loss = losses(
                    block(0, slot, u, HALF), block(1, slot, g, HALF), slot == 0 and flip == 0
                )
                u_scr[len(news) + i, u : u + HALF, :] += loss
                g_scr[slot, :, g : g + HALF] += columns(loss)

    if ins:
        pl.when(core == 0)(lambda: own(0))
        pl.when(core == 1)(lambda: own(1))
    u_out[...] = u_in[...]
    for i, slot in enumerate(u_slots):
        u_out[slot : slot + 1, :] += jnp.sum(u_scr[i].T, axis=0, keepdims=True)
    g_out[...] = g_in[...]
    for slot in g_slots:
        g_out[slot : slot + 1, :] += jnp.sum(g_scr[slot], axis=0, keepdims=True)


def tiles(where, us, gs, news, olds, ins, acc):
    pairs = len(news) * len(olds) + len(ins) ** 2 / 2
    operands, sides = [], []
    for arrays, slots in ((us, news + ins), (gs, olds + ins)):
        used = sorted({where[s][0] for s in slots})
        sides.append({s: (len(operands) + used.index(where[s][0]), where[s][1]) for s in slots})
        operands += [arrays[a] for a in used]
    vmem = pl.BlockSpec(memory_space=pltpu.VMEM)
    sums = jax.ShapeDtypeStruct((RING, ROWS), jnp.float32)
    return pl.pallas_call(
        functools.partial(tile_kernel, sides, news, olds, ins),
        out_shape=(sums, sums),
        in_specs=[vmem] * (len(operands) + 2),
        out_specs=(vmem, vmem),
        scratch_shapes=[
            pltpu.VMEM((len(news) + len(ins), ROWS, 128), jnp.float32),
            pltpu.VMEM((RING, 8, ROWS), jnp.float32),
        ],
        compiler_params=pltpu.CompilerParams(vmem_limit_bytes=16 * 2**20),
        cost_estimate=pl.CostEstimate(
            flops=int(pairs * 2 * ROWS * ROWS * DEPTH),
            bytes_accessed=2 * DEPTH * sum(o.shape[0] for o in operands),
            transcendentals=int(pairs * 2 * ROWS * ROWS),
        ),
        name="tiles",
    )(*operands, *acc)


def fold_kernel(mine, other, out):
    share, row = lax.axis_index("width"), lax.axis_index("row")
    y, z, x = row // (Z * X), row // X % Z, row % X
    spot = jnp.where(share % C == 0, z, jnp.where(y == 0, x, RING - 1 - x))
    scale = jnp.where(share < C, jnp.float32(1.0 / TOTAL), jnp.float32(-1.0 / TOTAL))
    for d, s in enumerate(SLOT):
        to = 2 * lax.rem(spot + d, RING)
        both = (mine[s : s + 1, :] + other[s : s + 1, :]) * scale
        for k in range(2):
            out[pl.ds(to + k, 1), :] = both[:, k * HALF : (k + 1) * HALF]


def fold(mine, other):
    vmem = pl.BlockSpec(memory_space=pltpu.VMEM)
    return pl.pallas_call(
        fold_kernel,
        out_shape=jax.ShapeDtypeStruct((2 * RING, HALF), jnp.float32),
        in_specs=[vmem, vmem],
        out_specs=vmem,
        compiler_params=pltpu.CompilerParams(vmem_limit_bytes=2**20),
        name="fold",
    )(mine, other)


def local(image_learner, image_reference, text_learner, text_reference):
    share = lax.axis_index("width")
    at_zero, low = share % C == 0, share < C

    il, ir, tl, tr = (a.T for a in (image_learner, image_reference, text_learner, text_reference))

    def pick(own_type, own_kind):
        image, text = (jnp.where(low == own_type, l, r) for l, r in ((il, ir), (tl, tr)))
        return jnp.where(at_zero == own_kind, image, text)

    tie = lax.optimization_barrier
    mine, p_away, q_away = tie(
        (pick(True, True), pick(True, False), jnp.stack([pick(False, True), pick(False, False)]))
    )

    def in_order(same, cross):
        return jnp.where(
            at_zero, jnp.concatenate([same, cross], 0), jnp.concatenate([cross, same], 0)
        )

    p0 = in_order(mine, send(p_away, CORES))
    q_same, q_cross = send(q_away, HALVES)
    q0 = in_order(q_same, send(q_cross, CORES))

    def step(f, b):
        b = send(b, BACK)
        return send(f, AHEAD), b

    zero = jnp.zeros((RING, ROWS), jnp.float32)
    acc = (zero, zero)
    us, gs, where = [], [], {}

    def add(slots, *blocks):
        u = prep(*blocks)
        for i, slot in enumerate(slots):
            where[slot] = (len(us), i * ROWS)
        us.append(u)
        gs.append(send(u, CORES))

    def work(acc, news, olds, ins):
        return tiles(where, us, gs, news, olds, ins, acc)

    p1 = step(p0, p0)
    q0, p1 = tie((q0, p1))
    q1 = step(q0, q0)
    p2 = step(*p1)
    q2 = step(*q1)
    q3 = step(*q2)
    q4 = send(q3[1], BACK)
    p3 = step(*p2)
    p4 = send(p3[0], AHEAD)
    p3, q3, p0, p1, p2, q0, q1, q2 = tie((p3, q3, p0, p1, p2, q0, q1, q2))
    add((0, 1, 2), (p0, q0), (p1[0], q1[0]), (p1[1], q1[1]))
    add((3, 4), (p2[0], q2[0]), (p2[1], q2[1]))
    acc = work(acc, (3, 4), (0, 1, 2), (0, 1, 2))
    add((5, 6), (p3[0], q3[0]), (p3[1], q3[1]))
    acc = work(acc, (5, 6), (0, 1, 2, 3, 4), (3, 4))
    acc = work(acc, (), (), (5, 6))
    p4, q4, acc = tie((p4, q4, acc))
    add((7,), (p4, q4))
    acc = work(acc, (7,), (0, 1, 2, 3, 4, 5, 6), ())
    u_acc, g_acc = work(acc, (), (), (7,))

    sums = fold(u_acc, send(g_acc, CORES))
    sums = lax.all_to_all(sums, AXES, 0, 0, axis_index_groups=GROUPS, tiled=True)
    sums = jnp.sum(sums, axis=0)
    mine = jnp.where(at_zero, sums[:64], sums[64:])
    other = send(jnp.where(at_zero, sums[64:], sums[:64]), CORES)
    return jnp.where(at_zero, mine, other), jnp.where(at_zero, other, mine)


def solution(mesh):
    spec = jax.sharding.PartitionSpec
    return jax.shard_map(
        local,
        mesh=mesh,
        in_specs=(spec("row", "width"),) * 4,
        out_specs=(spec(AXES),) * 2,
        check_vma=False,
    )
```

```python
import functools

import jax
import jax.numpy as jnp
import numpy as np
from jax import lax
from jax.experimental import pallas as pl
from jax.experimental.pallas import tpu as pltpu

AXES = ("row", "width")
Y, Z, X, H, C = 2, 8, 4, 2, 2
RING = 8
ROWS = 256
HALF = 128
DEPTH = 1152
QUARTER = 288
TOTAL = 16384
LOG2E = 1.4426950408889634
SLOT = (0, 2, 4, 6, 7, 5, 3, 1)


def device(y, z, x, h, c):
    return (((y * Z + z) * X + x) * H + h) * C + c


def place(p):
    p %= RING
    return (0, p) if p < X else (1, RING - 1 - p)


def route(d):
    pairs = []
    for y in range(Y):
        for z in range(Z):
            for x in range(X):
                ny, nx = place((x if y == 0 else RING - 1 - x) + d)
                for h in range(H):
                    pairs.append((device(y, z, x, h, 0), device(y, (z + d) % Z, x, h, 0)))
                    pairs.append((device(y, z, x, h, 1), device(ny, z, nx, h, 1)))
    return pairs


CORES = [(i, i ^ 1) for i in range(Y * Z * X * H * C)]
HALVES = [(i, i ^ 2) for i in range(Y * Z * X * H * C)]
AHEAD, BACK = route(1), route(-1)
GROUPS = [
    [device(y, z, x, h, 0) for h in range(H) for z in range(Z)] for y in range(Y) for x in range(X)
] + [
    [device(place(p)[0], z, place(p)[1], h, 1) for h in range(H) for p in range(RING)]
    for z in range(Z)
]


def send(x, route):
    return lax.ppermute(x, AXES, route)


def prep_kernel(n, *refs):
    ins, out, scr = refs[:-2], refs[-2], refs[-1]
    for b in range(n):
        parts = ins[2 * b : 2 * b + 2]
        acc = jnp.zeros((16, ROWS), jnp.float32)
        for part in parts:
            for r in range(0, part.shape[0], 16):
                v = part[r : r + 16, :].astype(jnp.float32)
                acc = acc + v * v
        inv = lax.rsqrt(jnp.sum(acc, axis=0, keepdims=True) + 1e-06)
        off = 0
        for part in parts:
            for r in range(0, part.shape[0], 16):
                v = part[r : r + 16, :].astype(jnp.float32)
                scr[off + r : off + r + 16, :] = (v * inv).astype(jnp.bfloat16)
            off += part.shape[0]
        for k in range(0, DEPTH, 128):
            out[b * ROWS : (b + 1) * ROWS, k : k + 128] = scr[k : k + 128, :].T


def prep(*blocks):
    n = len(blocks)
    vmem = pl.BlockSpec(memory_space=pltpu.VMEM)
    return pl.pallas_call(
        functools.partial(prep_kernel, n),
        out_shape=jax.ShapeDtypeStruct((n * ROWS, DEPTH), jnp.bfloat16),
        in_specs=[vmem] * (2 * n),
        out_specs=vmem,
        scratch_shapes=[pltpu.VMEM((DEPTH, ROWS), jnp.bfloat16)],
        compiler_params=pltpu.CompilerParams(vmem_limit_bytes=8 * 2**20),
        cost_estimate=pl.CostEstimate(
            flops=4 * n * ROWS * DEPTH, bytes_accessed=4 * n * ROWS * DEPTH, transcendentals=0
        ),
        name="prep",
    )(*[p for b in blocks for p in b])


def tile_kernel(where, news, olds, ins, *refs):
    u_in, g_in, u_out, g_out, u_scr, g_scr = refs[-6:]
    share = lax.axis_index("width")
    core, low = share % C, share < C
    scale = jnp.where(low, jnp.float32(40.0 * LOG2E), jnp.float32(20.0 * LOG2E))
    shift = jnp.where(low, jnp.float32(-2.0 * LOG2E), jnp.float32(-1.0 * LOG2E))
    u_slots, g_slots = news + ins, tuple(sorted(set(olds + ins)))
    u_scr[...] = jnp.zeros_like(u_scr)
    for slot in g_slots:
        g_scr[slot] = jnp.zeros_like(g_scr[slot])

    def block(side, slot, first=0, rows=ROWS):
        a, start = where[side][slot]
        return refs[a][start + first : start + first + rows, :]

    def losses(left, right, diag=False):
        v = lax.dot_general(
            left, right, (((1,), (1,)), ((), ())), preferred_element_type=jnp.float32
        )
        v = v * scale + shift
        if diag:
            row = lax.broadcasted_iota(jnp.int32, v.shape, 0)
            col = lax.broadcasted_iota(jnp.int32, v.shape, 1)
            v = jnp.where(row == col, -v, v)
        return jnp.log(1.0 + jnp.exp2(v))

    def rows(loss):
        return sum(loss[:, k : k + 128] for k in range(0, loss.shape[1], 128))

    def columns(loss):
        return jnp.sum(loss.reshape(loss.shape[0] // 8, 8, loss.shape[1]), axis=0)

    if news:
        left = jnp.concatenate([block(0, s) for s in news], axis=0)
        for sg in olds:
            loss = losses(left, block(1, sg))
            for i in range(len(news)):
                u_scr[i] += rows(loss[i * ROWS : (i + 1) * ROWS])
            g_scr[sg] += columns(loss)
    for j, su in enumerate(ins):
        for sg in ins[:j]:
            loss = losses(block(0, su), block(1, sg))
            u_scr[len(news) + j] += rows(loss)
            g_scr[sg] += columns(loss)

    def own(flip):
        for i, slot in enumerate(ins):
            for k in range(2):
                u, g = k * HALF, (k ^ flip) * HALF
                loss = losses(
                    block(0, slot, u, HALF), block(1, slot, g, HALF), slot == 0 and flip == 0
                )
                u_scr[len(news) + i, u : u + HALF, :] += loss
                g_scr[slot, :, g : g + HALF] += columns(loss)

    if ins:
        pl.when(core == 0)(lambda: own(0))
        pl.when(core == 1)(lambda: own(1))
    u_out[...] = u_in[...]
    for i, slot in enumerate(u_slots):
        u_out[slot : slot + 1, :] += jnp.sum(u_scr[i].T, axis=0, keepdims=True)
    g_out[...] = g_in[...]
    for slot in g_slots:
        g_out[slot : slot + 1, :] += jnp.sum(g_scr[slot], axis=0, keepdims=True)


def tiles(where, us, gs, news, olds, ins, acc):
    pairs = len(news) * len(olds) + len(ins) ** 2 / 2
    operands, sides = [], []
    for arrays, slots in ((us, news + ins), (gs, olds + ins)):
        used = sorted({where[s][0] for s in slots})
        sides.append({s: (len(operands) + used.index(where[s][0]), where[s][1]) for s in slots})
        operands += [arrays[a] for a in used]
    vmem = pl.BlockSpec(memory_space=pltpu.VMEM)
    sums = jax.ShapeDtypeStruct((RING, ROWS), jnp.float32)
    return pl.pallas_call(
        functools.partial(tile_kernel, sides, news, olds, ins),
        out_shape=(sums, sums),
        in_specs=[vmem] * (len(operands) + 2),
        out_specs=(vmem, vmem),
        scratch_shapes=[
            pltpu.VMEM((len(news) + len(ins), ROWS, 128), jnp.float32),
            pltpu.VMEM((RING, 8, ROWS), jnp.float32),
        ],
        compiler_params=pltpu.CompilerParams(vmem_limit_bytes=16 * 2**20),
        cost_estimate=pl.CostEstimate(
            flops=int(pairs * 2 * ROWS * ROWS * DEPTH),
            bytes_accessed=2 * DEPTH * sum(o.shape[0] for o in operands),
            transcendentals=int(pairs * 2 * ROWS * ROWS),
        ),
        name="tiles",
    )(*operands, *acc)


def fold_kernel(mine, other, out):
    share, row = lax.axis_index("width"), lax.axis_index("row")
    y, z, x = row // (Z * X), row // X % Z, row % X
    spot = jnp.where(share % C == 0, z, jnp.where(y == 0, x, RING - 1 - x))
    scale = jnp.where(share < C, jnp.float32(1.0 / TOTAL), jnp.float32(-1.0 / TOTAL))
    for d, s in enumerate(SLOT):
        to = lax.rem(spot + d, RING)
        both = (mine[s : s + 1, :] + other[s : s + 1, :]) * scale
        for k in range(2):
            out[pl.ds(k * RING + to, 1), :] = both[:, k * HALF : (k + 1) * HALF]


def fold(mine, other):
    vmem = pl.BlockSpec(memory_space=pltpu.VMEM)
    return pl.pallas_call(
        fold_kernel,
        out_shape=jax.ShapeDtypeStruct((2 * RING, HALF), jnp.float32),
        in_specs=[vmem, vmem],
        out_specs=vmem,
        compiler_params=pltpu.CompilerParams(vmem_limit_bytes=2**20),
        name="fold",
    )(mine, other)


def local(image_learner, image_reference, text_learner, text_reference):
    share = lax.axis_index("width")
    at_zero, low = share % C == 0, share < C

    il, ir, tl, tr = (a.T for a in (image_learner, image_reference, text_learner, text_reference))

    def pick(own_type, own_kind):
        image, text = (jnp.where(low == own_type, l, r) for l, r in ((il, ir), (tl, tr)))
        return jnp.where(at_zero == own_kind, image, text)

    tie = lax.optimization_barrier
    mine, p_away, q_away = tie(
        (pick(True, True), pick(True, False), jnp.stack([pick(False, True), pick(False, False)]))
    )

    def in_order(same, cross):
        return jnp.where(
            at_zero, jnp.concatenate([same, cross], 0), jnp.concatenate([cross, same], 0)
        )

    p0 = in_order(mine, send(p_away, CORES))
    q_same, q_cross = send(q_away, HALVES)
    q0 = in_order(q_same, send(q_cross, CORES))

    def step(f, b):
        b = send(b, BACK)
        return send(f, AHEAD), b

    zero = jnp.zeros((RING, ROWS), jnp.float32)
    acc = (zero, zero)
    us, gs, where = [], [], {}

    def add(slots, *blocks):
        u = prep(*blocks)
        for i, slot in enumerate(slots):
            where[slot] = (len(us), i * ROWS)
        us.append(u)
        gs.append(send(u, CORES))

    def work(acc, news, olds, ins):
        return tiles(where, us, gs, news, olds, ins, acc)

    p1 = step(p0, p0)
    q0, p1 = tie((q0, p1))
    q1 = step(q0, q0)
    p2 = step(*p1)
    q2 = step(*q1)
    p3 = step(*p2)
    q3 = step(*q2)
    p4 = send(p3[0], AHEAD)
    q4 = send(q3[1], BACK)
    p3, q3, p0, p1, p2, q0, q1, q2 = tie((p3, q3, p0, p1, p2, q0, q1, q2))
    add((0, 1, 2), (p0, q0), (p1[0], q1[0]), (p1[1], q1[1]))
    add((3, 4), (p2[0], q2[0]), (p2[1], q2[1]))
    acc = work(acc, (3, 4), (0, 1, 2), (0, 1, 2))
    add((5, 6), (p3[0], q3[0]), (p3[1], q3[1]))
    acc = work(acc, (5, 6), (0, 1, 2, 3, 4), (3, 4))
    p4, q4, acc = tie((p4, q4, acc))
    add((7,), (p4, q4))
    acc = work(acc, (7,), (0, 1, 2, 3, 4, 5, 6), (5, 6))
    u_acc, g_acc = work(acc, (), (), (7,))

    sums = fold(u_acc, send(g_acc, CORES))
    sums = lax.all_to_all(sums, AXES, 0, 0, axis_index_groups=GROUPS, tiled=True)
    sums = jnp.sum(sums, axis=0)
    mine = jnp.where(at_zero, sums[:64], sums[64:])
    other = send(jnp.where(at_zero, sums[64:], sums[:64]), CORES)
    return jnp.where(at_zero, mine, other), jnp.where(at_zero, other, mine)


def solution(mesh):
    spec = jax.sharding.PartitionSpec
    return jax.shard_map(
        local,
        mesh=mesh,
        in_specs=(spec("row", "width"),) * 4,
        out_specs=(spec(AXES),) * 2,
        check_vma=False,
    )
```
